512 devices in a mesh: row: 16 (over y, z_lo), col: 32 (over x, z_hi, core).
Axes of the slice: x: 4, y: 8, z: 8 (z_hi: 4, z_lo: 2; z = z_hi * 2 + z_lo), core: 2. Of those that a mesh axis runs over, the one named last changes fastest.
Arguments:
- tokens: bfloat16 [512, 12288], P('row', 'col'), may hold values from -6 to 6
- grad_out: bfloat16 [512, 12288], P('row', 'col'), may hold values from -1.796875 to 1.796875
- pre_act: bfloat16 [512, 24576], P('col', 'row'), may hold values from -6 to 6
- w_in: bfloat16 [24576, 12288], P('row', 'col'), may hold values from -0.0546875 to 0.0546875
- w_out: bfloat16 [24576, 12288], P('row', 'col'), may hold values from -0.0390625 to 0.0390625
Outputs:
- grad_tokens: bfloat16 [512, 12288], P('row', 'col')
- grad_w_in: bfloat16 [24576, 12288], P('row', 'col')
- grad_w_out: bfloat16 [24576, 12288], P('row', 'col')
The draws below stay inside these ranges and needn't reach their ends.
All inputs are finite; a program needn't handle non-finite values.
Results may differ from the reference program's by a relative error of at most 0.005.
Values may be sent and summed in bfloat16 or wider, within the bound.
A program may use at most 64 MiB of HBM per device.

```python
import jax
import jax.numpy as jnp
from jax import lax

D = 12288
H = 24576
TOKENS = 512


def block_levels(stream_key, dims, pieces, smallest, largest):
    level = 1.0
    for position, blocks in pieces:
        steps = jax.random.uniform(jax.random.fold_in(jax.random.fold_in(stream_key, 6), position), (blocks,), jnp.float32, smallest / len(pieces), largest / len(pieces))
        level = level * jnp.repeat(jnp.exp(steps), dims[position] // blocks).reshape((-1,) + (1,) * (len(dims) - 1 - position))
    return level


def gaussian(stream_key, extent, deviation, reach, split=(), dtype=jnp.bfloat16):
    entries = jax.random.normal(stream_key, extent, jnp.float32) * deviation
    if len(split) > 0:
        entries = block_levels(stream_key, extent, split, -0.22, 0.18) * entries
    return jnp.clip(entries, min=-reach, max=reach).astype(dtype)


def setup_inputs(seed: int = 0) -> dict:
    splits = jax.random.split(jax.random.key(seed), 6)
    tokens = gaussian(splits[0], (TOKENS, D), 1.0, 6.0, ((0, 16), (1, 32)))
    grad_out = gaussian(splits[1], (TOKENS, D), 0.3, 1.796875, ((0, 16), (1, 32)))
    pre_act = gaussian(splits[2], (TOKENS, H), 1.0, 6.0, ((0, 32), (1, 16)))
    w_in = gaussian(splits[3], (H, D), D ** -0.5, 0.0546875, ((0, 16), (1, 32)))
    w_out = gaussian(splits[4], (H, D), H ** -0.5, 0.0390625, ((0, 16), (1, 32)))
    return dict(tokens=tokens, grad_out=grad_out, pre_act=pre_act, w_in=w_in, w_out=w_out)


tanh_scale = 0.7978845608028654
cubic_term = 0.044715


def gelu_parts(pre_act):
    pre_value = pre_act.astype(jnp.float32)
    tanh_arg = tanh_scale * (pre_value + cubic_term * pre_value * pre_value * pre_value)
    tangent = jnp.tanh(tanh_arg)
    hidden_value = 0.5 * pre_value * (1.0 + tangent)
    gelu_slope = 0.5 * (1.0 + tangent) + 0.5 * pre_value * (1.0 - tangent * tangent) * tanh_scale * (1.0 + 3.0 * cubic_term * pre_value * pre_value)
    return hidden_value, gelu_slope


def reference(tokens, grad_out, pre_act, w_in, w_out):
    contract_rows = (((0,), (0,)), ((), ()))
    contract_cols = (((1,), (1,)), ((), ()))
    grad_hidden = lax.dot_general(grad_out, w_out, contract_cols, preferred_element_type=jnp.float32)
    hidden_value, gelu_slope = gelu_parts(pre_act)
    hidden = hidden_value.astype(jnp.bfloat16)
    grad_pre = (grad_hidden * gelu_slope).astype(jnp.bfloat16)
    grad_tokens = jnp.dot(grad_pre, w_in, preferred_element_type=jnp.float32).astype(jnp.bfloat16)
    grad_w_in = lax.dot_general(grad_pre, tokens, contract_rows, preferred_element_type=jnp.float32).astype(jnp.bfloat16)
    grad_w_out = lax.dot_general(hidden, grad_out, contract_rows, preferred_element_type=jnp.float32).astype(jnp.bfloat16)
    return (grad_tokens, grad_w_in, grad_w_out)
```

```python
import jax
import jax.numpy as jnp
from jax import lax
from jax.experimental import pallas as pl
from jax.experimental.pallas import tpu as pltpu
from jax.sharding import PartitionSpec as P

tanh_scale = 0.7978845608028654
cubic_term = 0.044715

MESH = pl.DeviceIdType.MESH
F32 = jnp.float32
BF16 = jnp.bfloat16
NX, NZ, NY = 4, 4, 8
FEAT = 384
HID = 1536
HQ = HID // NX
FAR_FIRST = (4, 3, 5, 2, 6, 1, 7)
NEAR_FIRST = (1, 7, 2, 6, 3, 5, 4)
X_ORDER = (2, 1, 3)
Z_ORDER = (2, 1, 3)


def gelu_hidden(u):
    q = jnp.tanh(tanh_scale * (u + cubic_term * u * u * u))
    return 0.5 * u * (1.0 + q)


def gelu_slope(u):
    q = jnp.tanh(tanh_scale * (u + cubic_term * u * u * u))
    return 0.5 * (1.0 + q) + 0.5 * u * (1.0 - q * q) * tanh_scale * (1.0 + 3.0 * cubic_term * u * u)


def kernel(
    tok_hbm, go_hbm, pre_hbm, win_hbm, wout_hbm,
    gt_hbm, gwi_hbm, gwo_hbm,
    tok_own, go_own, pre_own, wo2, wi2, go, go_sib, tok, pre, part, part_f, rx, sb, rz,
    gp, gp_sib, hid, hid_sib, fb, gz, gb, gy, gt_out, gwi_out, gwo_out,
    local, a_s, a_r, az_s, az_r, x_s, x_r, z_s, z_r, p_s, p_r, hz_s, hz_r, hx_s, hx_r,
    ez_s, ez_r, ex_s, ex_r, gz_s, gz_r, gy_s, gy_r, t_s, t_r, tz_s, tz_r, c_s, c_r,
):
    r, c = lax.axis_index("row"), lax.axis_index("col")
    y, zl = r // 2, r % 2
    x, zh, k = c // 8, (c // 2) % NZ, c % 2

    def dev(dy=0, dzl=0, dx=0, dz=0, core=None):
        yy, ll = (y + dy) % NY, (zl + dzl) % 2
        xx, hh = (x + dx) % NX, (zh + dz) % NZ
        kk = k if core is None else core
        return (yy * 2 + ll, (xx * NZ + hh) * 2 + kk)

    def slot(yy, ll):
        return ((yy % 2) * 2 + ll) * NX + yy // 2

    def rows(start, size):
        return pl.ds(pl.multiple_of(start, 16), size)

    def cols(index, size):
        return pl.ds(pl.multiple_of(index * size, 128), size)

    sends = []

    def send(src, dst, ssem, rsem, to):
        cp = pltpu.make_async_remote_copy(
            src_ref=src, dst_ref=dst, send_sem=ssem, recv_sem=rsem, device_id=to, device_id_type=MESH
        )
        cp.start()
        sends.append((src, ssem))

    def arrived(ref, sem):
        pltpu.make_async_copy(ref, ref, sem).wait()

    sib = dev(core=1 - k)
    mine = slot(y, zl)

    peers = [dev(dy=d, core=kk) for d in range(1, NY) for kk in range(2)]
    peers += [dev(dzl=1, core=kk) for kk in range(2)] + [sib]
    peers += [dev(dx=d) for d in range(1, NX)] + [dev(dz=d) for d in range(1, NZ)]
    barrier = pltpu.get_barrier_semaphore()
    for to in peers:
        pl.semaphore_signal(barrier, inc=1, device_id=to, device_id_type=MESH)

    loads = [
        pltpu.make_async_copy(pre_hbm, pre_own, local.at[0]),
        pltpu.make_async_copy(go_hbm, go_own, local.at[1]),
        pltpu.make_async_copy(tok_hbm, tok_own, local.at[2]),
        pltpu.make_async_copy(wout_hbm, wo2.at[:, cols(k, FEAT)], local.at[3]),
        pltpu.make_async_copy(win_hbm, wi2.at[:, cols(k, FEAT)], local.at[4]),
    ]
    for cp in loads:
        cp.start()
    loads[0].wait()
    loads[1].wait()
    my_rows = rows(16 * (zh * NX + x), 16)
    hid[my_rows, :] = gelu_hidden(pre_own[...].astype(F32)).astype(BF16)
    pre[rows(16 * x, 16), :] = pre_own[:, cols(x, HQ)]
    go[rows(16 * mine, 16), cols(k, FEAT)] = go_own[k]
    pl.semaphore_wait(barrier, len(peers))

    send(go_own.at[1 - k], go.at[rows(16 * mine, 16), cols(k, FEAT)], c_s.at[0], c_r.at[0], sib)
    for d in FAR_FIRST:
        for kk in range(2):
            send(go_own.at[kk], go.at[rows(16 * mine, 16), cols(k, FEAT)], a_s.at[d, kk], a_r.at[d], dev(dy=d, core=kk))
    for kk in range(2):
        send(go_own.at[kk], go.at[rows(16 * mine, 16), cols(k, FEAT)], az_s.at[0, kk], az_r.at[0], dev(dzl=1, core=kk))
    send(wout_hbm, wo2.at[:, cols(k, FEAT)], c_s.at[1], c_r.at[1], sib)
    for d in X_ORDER:
        send(pre_own.at[:, cols((x + d) % NX, HQ)], pre.at[rows(16 * x, 16), :], p_s.at[d], p_r.at[d], dev(dx=d))
    for d in Z_ORDER:
        send(hid.at[my_rows], hid.at[my_rows], hz_s.at[d], hz_r.at[d], dev(dz=d))
    for d in X_ORDER:
        send(hid.at[my_rows], hid.at[my_rows], hx_s.at[0, d], hx_r.at[0, d], dev(dx=d))
    for d in NEAR_FIRST:
        block = go.at[rows(16 * slot((y - d) % NY, zl), 16), :]
        arrived(block, a_r.at[d])
        send(block, block, az_s.at[d, 0], az_r.at[d], dev(dzl=1))
    arrived(go.at[rows(16 * mine, 16), cols(1 - k, FEAT)], c_r.at[0])
    loads[3].wait()
    arrived(wo2.at[:, cols(1 - k, FEAT)], c_r.at[1])
    for d in (0,) + NEAR_FIRST:
        arrived(go.at[rows(16 * slot((y - d) % NY, 1 - zl), 16), :], az_r.at[d])

    for dz in Z_ORDER + (0,):
        t = rows(64 * ((zh + dz) % NZ), 64)
        for dx in X_ORDER + (0,):
            xx = (x + dx) % NX
            product = lax.dot_general(
                go[t, :], wo2[rows(HQ * xx, HQ), :], (((1,), (1,)), ((), ())), preferred_element_type=F32
            )
            if dx:
                part[xx, t, :] = product.astype(BF16)
                send(part.at[xx, t], rx.at[dx - 1, t], x_s.at[dz, dx], x_r.at[dz, dx], dev(dx=dx))
            else:
                part_f[t, :] = product

    send(go.at[:, cols(1 - k, FEAT)], go_sib, c_s.at[2], c_r.at[2], sib)
    send(win_hbm, wi2.at[:, cols(k, FEAT)], c_s.at[3], c_r.at[3], sib)
    loads[2].wait()
    tok[mine] = tok_own[...]
    for d in FAR_FIRST:
        send(tok_own, tok.at[mine], t_s.at[d], t_r.at[d], dev(dy=d))
    send(tok_own, tok.at[mine], tz_s.at[0], tz_r.at[0], dev(dzl=1))

    for dz in Z_ORDER + (0,):
        t = rows(64 * ((zh + dz) % NZ), 64)
        for dx in X_ORDER:
            arrived(rx.at[dx - 1, t], x_r.at[dz, dx])
        total = part_f[t, :] + rx[0, t, :].astype(F32) + rx[1, t, :].astype(F32) + rx[2, t, :].astype(F32)
        if dz:
            sb[dz - 1] = total.astype(BF16)
            send(sb.at[dz - 1], rz.at[dz - 1], z_s.at[dz], z_r.at[dz], dev(dz=dz))
        else:
            part_f[t, :] = total

    for dz in (1, 3, 2):
        block = hid.at[rows(16 * (((zh - dz) % NZ) * NX + x), 16)]
        arrived(block, hz_r.at[dz])
        for dx in X_ORDER:
            send(block, block, hx_s.at[dz, dx], hx_r.at[dz, dx], dev(dx=dx))

    for d in X_ORDER:
        arrived(pre.at[rows(16 * ((x - d) % NX), 16), :], p_r.at[d])
    slope = gelu_slope(pre[...].astype(F32))
    for d in (1, 3, 2):
        arrived(rz.at[d - 1], z_r.at[d])
    t = rows(64 * zh, 64)
    total = part_f[t, :] + rz[0].astype(F32) + rz[1].astype(F32) + rz[2].astype(F32)
    gp[t, cols(x, HQ)] = (total * slope).astype(BF16)

    block = gp.at[t, cols(x, HQ)]
    for d in Z_ORDER:
        send(block, block, ez_s.at[d], ez_r.at[d], dev(dz=d))
    for d in X_ORDER:
        send(block, block, ex_s.at[0, d], ex_r.at[0, d], dev(dx=d))
    for d in NEAR_FIRST:
        block = tok.at[slot((y - d) % NY, zl)]
        arrived(block, t_r.at[d])
        send(block, block, tz_s.at[d], tz_r.at[d], dev(dzl=1))
    for dz in (1, 3, 2):
        block = gp.at[rows(64 * ((zh - dz) % NZ), 64), cols(x, HQ)]
        arrived(block, ez_r.at[dz])
        for dx in X_ORDER:
            send(block, block, ex_s.at[dz, dx], ex_r.at[dz, dx], dev(dx=dx))

    for dz in range(NZ):
        for dx in X_ORDER:
            arrived(hid.at[rows(16 * (((zh - dz) % NZ) * NX + (x - dx) % NX), 16)], hx_r.at[dz, dx])
    send(hid, hid_sib, c_s.at[4], c_r.at[4], sib)

    loads[4].wait()
    arrived(wi2.at[:, cols(1 - k, FEAT)], c_r.at[3])

    def grad_tokens_part(wave):
        t = rows(64 * wave, 64)
        dz = (zh - wave) % NZ
        for dx in X_ORDER:
            arrived(gp.at[t, cols((x - dx) % NX, HQ)], ex_r.at[dz, dx])
        return jnp.dot(gp[t, :], wi2[...], preferred_element_type=F32)

    for odd in (1, 0):
        fb[odd] = grad_tokens_part((1 - zl) + 2 * ((y + odd) % 2)).astype(BF16)
        send(fb.at[odd], gz.at[odd], gz_s.at[odd], gz_r.at[odd], dev(dzl=1))
    for odd in (1, 0):
        mine_part = grad_tokens_part(zl + 2 * ((y + odd) % 2))
        arrived(gz.at[odd], gz_r.at[odd])
        gb[odd] = (mine_part + gz[odd].astype(F32)).astype(BF16)
        for d in ((3, 5, 1, 7) if odd else (4, 2, 6)):
            t = rows(16 * (((y + d) % NY) // 2), 16)
            for kk in range(2):
                send(
                    gb.at[odd, t, pl.ds(FEAT * kk, FEAT)], gy.at[d, k], gy_s.at[d, kk], gy_r.at[d], dev(dy=d, core=kk)
                )
        if not odd:
            t = rows(16 * (y // 2), 16)
            gy[0, k] = gb[0, t, cols(k, FEAT)]
            send(gb.at[0, t, cols(1 - k, FEAT)], gy.at[0, k], gy_s.at[0, 0], gy_r.at[0], sib)
    send(gp, gp_sib, c_s.at[5], c_r.at[5], sib)

    over_tokens = (((0,), (0,)), ((), ()))
    arrived(go_sib, c_r.at[2])
    arrived(hid_sib, c_r.at[4])
    for h in range(0, HID, 256):
        a = lax.dot_general(hid[:, h : h + 256], go[:, cols(k, FEAT)], over_tokens, preferred_element_type=F32)
        b = lax.dot_general(hid_sib[:, h : h + 256], go_sib[...], over_tokens, preferred_element_type=F32)
        gwo_out[h : h + 256, :] = (a + b).astype(BF16)
    store_gwo = pltpu.make_async_copy(gwo_out, gwo_hbm, local.at[5])
    store_gwo.start()
    for d in (0,) + NEAR_FIRST:
        arrived(tok.at[slot((y - d) % NY, 1 - zl)], tz_r.at[d])
    arrived(gp_sib, c_r.at[5])
    tok_mine = tok[:, k].reshape(256, FEAT)
    tok_other = tok[:, 1 - k].reshape(256, FEAT)
    for h in range(0, HID, 256):
        a = lax.dot_general(gp[:, h : h + 256], tok_mine, over_tokens, preferred_element_type=F32)
        b = lax.dot_general(gp_sib[:, h : h + 256], tok_other, over_tokens, preferred_element_type=F32)
        gwi_out[h : h + 256, :] = (a + b).astype(BF16)
    store_gwi = pltpu.make_async_copy(gwi_out, gwi_hbm, local.at[6])
    store_gwi.start()

    arrived(gy.at[0, 1 - k], gy_r.at[0])
    total = gy[0].astype(F32)
    for d in NEAR_FIRST:
        arrived(gy.at[d], gy_r.at[d])
        total += gy[d].astype(F32)
    gt_out[...] = total.astype(BF16)
    store_gt = pltpu.make_async_copy(gt_out, gt_hbm, local.at[7])
    store_gt.start()
    for src, ssem in sends:
        arrived(src, ssem)
    store_gwo.wait()
    store_gwi.wait()
    store_gt.wait()


def per_device(tokens, grad_out, pre_act, w_in, w_out):
    vmem = pltpu.VMEM
    dma = pltpu.SemaphoreType.DMA
    any_space = pl.BlockSpec(memory_space=pl.ANY)
    scratch = [
        vmem((2, 16, FEAT), BF16),
        vmem((2, 16, FEAT), BF16),
        vmem((16, HID), BF16),
        vmem((HID, 2 * FEAT), BF16),
        vmem((HID, 2 * FEAT), BF16),
        vmem((256, 2 * FEAT), BF16),
        vmem((256, FEAT), BF16),
        vmem((16, 2, 16, FEAT), BF16),
        vmem((64, HQ), BF16),
        vmem((NX, 256, HQ), BF16),
        vmem((256, HQ), F32),
        vmem((NX - 1, 256, HQ), BF16),
        vmem((NZ - 1, 64, HQ), BF16),
        vmem((NZ - 1, 64, HQ), BF16),
        vmem((256, HID), BF16),
        vmem((256, HID), BF16),
        vmem((256, HID), BF16),
        vmem((256, HID), BF16),
        vmem((2, 64, 2 * FEAT), BF16),
        vmem((2, 64, 2 * FEAT), BF16),
        vmem((2, 64, 2 * FEAT), BF16),
        vmem((NY, 2, 16, FEAT), BF16),
        vmem((2, 16, FEAT), BF16),
        vmem((HID, FEAT), BF16),
        vmem((HID, FEAT), BF16),
        dma((8,)),
        dma((NY, 2)), dma((NY,)),
        dma((NY, 2)), dma((NY,)),
        dma((NZ, NX)), dma((NZ, NX)),
        dma((NZ,)), dma((NZ,)),
        dma((NX,)), dma((NX,)),
        dma((NZ,)), dma((NZ,)),
        dma((NZ, NX)), dma((NZ, NX)),
        dma((NZ,)), dma((NZ,)),
        dma((NZ, NX)), dma((NZ, NX)),
        dma((2,)), dma((2,)),
        dma((NY, 2)), dma((NY,)),
        dma((NY,)), dma((NY,)),
        dma((NY,)), dma((NY,)),
        dma((6,)), dma((6,)),
    ]
    grad_tokens, grad_w_in, grad_w_out = pl.pallas_call(
        kernel,
        out_shape=(
            jax.ShapeDtypeStruct((2, 16, FEAT), BF16),
            jax.ShapeDtypeStruct((HID, FEAT), BF16),
            jax.ShapeDtypeStruct((HID, FEAT), BF16),
        ),
        in_specs=[any_space] * 5,
        out_specs=(any_space,) * 3,
        scratch_shapes=scratch,
        compiler_params=pltpu.CompilerParams(
            collective_id=0, has_side_effects=True, vmem_limit_bytes=40 * 2**20
        ),
    )(tokens.reshape(2, 16, FEAT), grad_out.reshape(2, 16, FEAT), pre_act, w_in, w_out)
    return grad_tokens.reshape(32, FEAT), grad_w_in, grad_w_out


def solution(mesh):
    in_specs = (P("row", "col"), P("row", "col"), P("col", "row"), P("row", "col"), P("row", "col"))
    out_specs = (P("row", "col"), P("row", "col"), P("row", "col"))
    return jax.shard_map(per_device, mesh=mesh, in_specs=in_specs, out_specs=out_specs, check_vma=False)
```

```python
import jax
import jax.numpy as jnp
from jax import lax
from jax.experimental import pallas as pl
from jax.experimental.pallas import tpu as pltpu
from jax.sharding import PartitionSpec as P

tanh_scale = 0.7978845608028654
cubic_term = 0.044715

MESH = pl.DeviceIdType.MESH
F32 = jnp.float32
BF16 = jnp.bfloat16
NX, NZ, NY = 4, 4, 8
FEAT = 384
HID = 1536
HQ = HID // NX
FAR_FIRST = (4, 3, 5, 2, 6, 1, 7)
Y_ODD = (3, 5, 1, 7)
Y_EVEN = (4, 2, 6)
X_ORDER = (2, 1, 3)
Z_ORDER = (2, 1, 3)


def gelu_hidden(u):
    q = jnp.tanh(tanh_scale * (u + cubic_term * u * u * u))
    return 0.5 * u * (1.0 + q)


def gelu_slope(u):
    q = jnp.tanh(tanh_scale * (u + cubic_term * u * u * u))
    return 0.5 * (1.0 + q) + 0.5 * u * (1.0 - q * q) * tanh_scale * (1.0 + 3.0 * cubic_term * u * u)


def kernel(
    tok_hbm, go_hbm, pre_hbm, win_hbm, wout_hbm,
    gt_out, gwi_out, gwo_out,
    tok_own, go_own, pre_own, wo2, wi2, go, go_sib, tok, pre, part, part_f, rx, sb, rz,
    gp, gp_sib, hid, hid_sib, fb, gy,
    local, a_s, a_r, az_s, az_r, x_s, x_r, z_s, z_r, p_s, p_r, hz_s, hz_r, hx_s, hx_r,
    ez_s, ez_r, ex_s, ex_r, gy_s, gy_r, t_s, t_r, tz_s, tz_r, c_s, c_r,
):
    r, c = lax.axis_index("row"), lax.axis_index("col")
    y, zl = r // 2, r % 2
    x, zh, k = c // 8, (c // 2) % NZ, c % 2

    def dev(dy=0, dzl=0, dx=0, dz=0, core=None):
        yy, ll = (y + dy) % NY, (zl + dzl) % 2
        xx, hh = (x + dx) % NX, (zh + dz) % NZ
        kk = k if core is None else core
        return (yy * 2 + ll, (xx * NZ + hh) * 2 + kk)

    def slot(yy, ll):
        return ((yy % 2) * 2 + ll) * NX + yy // 2

    def rows(start, size):
        return pl.ds(pl.multiple_of(start, 16), size)

    def cols(index, size):
        return pl.ds(pl.multiple_of(index * size, 128), size)

    sends = []

    def send(src, dst, ssem, rsem, to):
        cp = pltpu.make_async_remote_copy(
            src_ref=src, dst_ref=dst, send_sem=ssem, recv_sem=rsem, device_id=to, device_id_type=MESH
        )
        cp.start()
        sends.append((src, ssem))

    def arrived(ref, sem):
        pltpu.make_async_copy(ref, ref, sem).wait()

    sib = dev(core=1 - k)
    mine = slot(y, zl)

    peers = [dev(dy=d, core=kk) for d in range(1, NY) for kk in range(2)]
    peers += [dev(dzl=1, core=kk) for kk in range(2)] + [sib]
    peers += [dev(dx=d) for d in range(1, NX)] + [dev(dz=d) for d in range(1, NZ)]
    barrier = pltpu.get_barrier_semaphore()
    for to in peers:
        pl.semaphore_signal(barrier, inc=1, device_id=to, device_id_type=MESH)

    loads = [
        pltpu.make_async_copy(pre_hbm, pre_own, local.at[0]),
        pltpu.make_async_copy(go_hbm, go_own, local.at[1]),
        pltpu.make_async_copy(tok_hbm, tok_own, local.at[2]),
        pltpu.make_async_copy(wout_hbm, wo2.at[:, cols(k, FEAT)], local.at[3]),
        pltpu.make_async_copy(win_hbm, wi2.at[:, cols(k, FEAT)], local.at[4]),
    ]
    for cp in loads:
        cp.start()
    loads[0].wait()
    loads[1].wait()
    my_rows = rows(16 * (zh * NX + x), 16)
    hid[my_rows, :] = gelu_hidden(pre_own[...].astype(F32)).astype(BF16)
    pre[rows(16 * x, 16), :] = pre_own[:, cols(x, HQ)]
    go[rows(16 * mine, 16), cols(k, FEAT)] = go_own[k]
    pl.semaphore_wait(barrier, len(peers))

    send(wout_hbm, wo2.at[:, cols(k, FEAT)], c_s.at[1], c_r.at[1], sib)
    send(go_own.at[1 - k], go.at[rows(16 * mine, 16), cols(k, FEAT)], c_s.at[0], c_r.at[0], sib)
    for d in Y_ODD + Y_EVEN:
        for kk in range(2):
            send(go_own.at[kk], go.at[rows(16 * mine, 16), cols(k, FEAT)], a_s.at[d, kk], a_r.at[d], dev(dy=d, core=kk))
    for kk in range(2):
        send(go_own.at[kk], go.at[rows(16 * mine, 16), cols(k, FEAT)], az_s.at[0, kk], az_r.at[0], dev(dzl=1, core=kk))
    for d in Z_ORDER:
        send(hid.at[my_rows], hid.at[my_rows], hz_s.at[d], hz_r.at[d], dev(dz=d))
    for d in X_ORDER:
        send(pre_own.at[:, cols((x + d) % NX, HQ)], pre.at[rows(16 * x, 16), :], p_s.at[d], p_r.at[d], dev(dx=d))
    for d in X_ORDER:
        send(hid.at[my_rows], hid.at[my_rows], hx_s.at[0, d], hx_r.at[0, d], dev(dx=d))

    def zh_of(wave):
        return ((y + 1 - wave % 2) % 2) * 2 + (zl + wave // 2) % 2

    for wave in range(4):
        for d in Y_ODD if wave % 2 == 0 else Y_EVEN:
            block = go.at[rows(16 * slot((y + NY - d) % NY, (zl + wave // 2) % 2), 16), :]
            if wave < 2:
                arrived(block, a_r.at[d])
                send(block, block, az_s.at[d, 0], az_r.at[d], dev(dzl=1))
            else:
                arrived(block, az_r.at[d])
        if wave == 0:
            loads[3].wait()
            arrived(wo2.at[:, cols(1 - k, FEAT)], c_r.at[1])
        if wave == 1:
            arrived(go.at[rows(16 * mine, 16), cols(1 - k, FEAT)], c_r.at[0])
        if wave == 3:
            arrived(go.at[rows(16 * slot(y, 1 - zl), 16), :], az_r.at[0])
        t = rows(64 * zh_of(wave), 64)
        for dx in X_ORDER + (0,):
            xx = (x + dx) % NX
            product = lax.dot_general(
                go[t, :], wo2[rows(HQ * xx, HQ), :], (((1,), (1,)), ((), ())), preferred_element_type=F32
            )
            if dx:
                part[xx, t, :] = product.astype(BF16)
                send(part.at[xx, t], rx.at[dx - 1, t], x_s.at[wave, dx], x_r.at[wave, dx], dev(dx=dx))
            else:
                part_f[t, :] = product

    send(go.at[:, cols(1 - k, FEAT)], go_sib, c_s.at[2], c_r.at[2], sib)
    send(win_hbm, wi2.at[:, cols(k, FEAT)], c_s.at[3], c_r.at[3], sib)
    loads[2].wait()
    tok[mine] = tok_own[...]
    for d in FAR_FIRST:
        send(tok_own, tok.at[mine], t_s.at[d], t_r.at[d], dev(dy=d))
    send(tok_own, tok.at[mine], tz_s.at[0], tz_r.at[0], dev(dzl=1))

    my_wave = ((zh + zl) % 2) * 2 + (zh // 2 + y + 1) % 2

    def other(index):
        return index + jnp.where(index >= my_wave, 1, 0)

    def summed_over_x(wave):
        t = rows(64 * zh_of(wave), 64)
        for dx in X_ORDER:
            arrived(rx.at[dx - 1, t], x_r.at[wave, dx])
        return part_f[t, :] + rx[0, t, :].astype(F32) + rx[1, t, :].astype(F32) + rx[2, t, :].astype(F32)

    for index in range(3):
        wave = other(index)
        sb[index] = summed_over_x(wave).astype(BF16)
        dz = (zh_of(wave) + NZ - zh) % NZ
        send(sb.at[index], rz.at[dz - 1], z_s.at[dz], z_r.at[dz], dev(dz=dz))
    total = summed_over_x(my_wave)

    for dz in (1, 3, 2):
        block = hid.at[rows(16 * (((zh + NZ - dz) % NZ) * NX + x), 16)]
        arrived(block, hz_r.at[dz])
        for dx in X_ORDER:
            send(block, block, hx_s.at[dz, dx], hx_r.at[dz, dx], dev(dx=dx))

    for d in X_ORDER:
        arrived(pre.at[rows(16 * ((x + NX - d) % NX), 16), :], p_r.at[d])
    slope = gelu_slope(pre[...].astype(F32))
    for d in (1, 3, 2):
        arrived(rz.at[d - 1], z_r.at[d])
    t = rows(64 * zh, 64)
    total += rz[0].astype(F32) + rz[1].astype(F32) + rz[2].astype(F32)
    gp[t, cols(x, HQ)] = (total * slope).astype(BF16)

    block = gp.at[t, cols(x, HQ)]
    for d in Z_ORDER:
        send(block, block, ez_s.at[d], ez_r.at[d], dev(dz=d))
    for d in X_ORDER:
        send(block, block, ex_s.at[0, d], ex_r.at[0, d], dev(dx=d))
    for d in FAR_FIRST:
        block = tok.at[slot((y + NY - d) % NY, zl)]
        arrived(block, t_r.at[d])
        send(block, block, tz_s.at[d], tz_r.at[d], dev(dzl=1))
    for index in range(3):
        origin = zh_of(other(index))
        dz = (zh + NZ - origin) % NZ
        block = gp.at[rows(64 * origin, 64), cols(x, HQ)]
        arrived(block, ez_r.at[dz])
        for dx in X_ORDER:
            send(block, block, ex_s.at[dz, dx], ex_r.at[dz, dx], dev(dx=dx))

    for dz in range(NZ):
        for dx in X_ORDER:
            arrived(hid.at[rows(16 * (((zh + NZ - dz) % NZ) * NX + (x + NX - dx) % NX), 16)], hx_r.at[dz, dx])
    send(hid, hid_sib, c_s.at[4], c_r.at[4], sib)

    loads[4].wait()
    arrived(wi2.at[:, cols(1 - k, FEAT)], c_r.at[3])
    for wave in range(4):
        zw = zh_of(wave)
        t = rows(64 * zw, 64)
        dz = (zh + NZ - zw) % NZ
        for dx in X_ORDER:
            arrived(gp.at[t, cols((x + NX - dx) % NX, HQ)], ex_r.at[dz, dx])
        fb[wave] = jnp.dot(gp[t, :], wi2[...], preferred_element_type=F32).astype(BF16)
        far = wave // 2
        for d in Y_ODD if wave % 2 == 0 else Y_EVEN + (0,):
            at = rows(16 * (((y + d) % NY) // 2), 16)
            for flip in range(2):
                kk = k if flip == 0 else 1 - k
                src = fb.at[wave, at, cols(kk, FEAT)]
                if d or far or flip:
                    send(src, gy.at[far, d, k], gy_s.at[far, d, flip], gy_r.at[far, d], dev(dy=d, dzl=far, core=kk))
                else:
                    gy[0, 0, k] = fb[wave, at, cols(kk, FEAT)]
    send(gp, gp_sib, c_s.at[5], c_r.at[5], sib)

    over_tokens = (((0,), (0,)), ((), ()))
    arrived(go_sib, c_r.at[2])
    arrived(hid_sib, c_r.at[4])
    for h in range(0, HID, 256):
        a = lax.dot_general(hid[:, h : h + 256], go[:, cols(k, FEAT)], over_tokens, preferred_element_type=F32)
        b = lax.dot_general(hid_sib[:, h : h + 256], go_sib[...], over_tokens, preferred_element_type=F32)
        gwo_out[h : h + 256, :] = (a + b).astype(BF16)
    for d in (0,) + FAR_FIRST:
        arrived(tok.at[slot((y + NY - d) % NY, 1 - zl)], tz_r.at[d])
    arrived(gp_sib, c_r.at[5])
    tok_mine = tok[:, k].reshape(256, FEAT)
    tok_other = tok[:, 1 - k].reshape(256, FEAT)
    for h in range(0, HID, 256):
        a = lax.dot_general(gp[:, h : h + 256], tok_mine, over_tokens, preferred_element_type=F32)
        b = lax.dot_general(gp_sib[:, h : h + 256], tok_other, over_tokens, preferred_element_type=F32)
        gwi_out[h : h + 256, :] = (a + b).astype(BF16)

    arrived(gy.at[0, 0, 1 - k], gy_r.at[0, 0])
    total = gy[0, 0].astype(F32)
    for far in range(2):
        for d in Y_ODD + Y_EVEN + ((0,) if far else ()):
            arrived(gy.at[far, d], gy_r.at[far, d])
            total += gy[far, d].astype(F32)
    gt_out[...] = total.astype(BF16)
    for src, ssem in sends:
        arrived(src, ssem)


def store_kernel(*refs):
    sem = refs[-1]
    copies = [pltpu.make_async_copy(refs[i], refs[3 + i], sem.at[i]) for i in range(3)]
    for cp in copies:
        cp.start()
    for cp in copies:
        cp.wait()


def per_device(tokens, grad_out, pre_act, w_in, w_out):
    vmem = pltpu.VMEM
    dma = pltpu.SemaphoreType.DMA
    any_space = pl.BlockSpec(memory_space=pl.ANY)
    scratch = [
        vmem((2, 16, FEAT), BF16),
        vmem((2, 16, FEAT), BF16),
        vmem((16, HID), BF16),
        vmem((HID, 2 * FEAT), BF16),
        vmem((HID, 2 * FEAT), BF16),
        vmem((256, 2 * FEAT), BF16),
        vmem((256, FEAT), BF16),
        vmem((16, 2, 16, FEAT), BF16),
        vmem((64, HQ), BF16),
        vmem((NX, 256, HQ), BF16),
        vmem((256, HQ), F32),
        vmem((NX - 1, 256, HQ), BF16),
        vmem((NZ - 1, 64, HQ), BF16),
        vmem((NZ - 1, 64, HQ), BF16),
        vmem((256, HID), BF16),
        vmem((256, HID), BF16),
        vmem((256, HID), BF16),
        vmem((256, HID), BF16),
        vmem((4, 64, 2 * FEAT), BF16),
        vmem((2, NY, 2, 16, FEAT), BF16),
        dma((5,)),
        dma((NY, 2)), dma((NY,)),
        dma((NY, 2)), dma((NY,)),
        dma((NZ, NX)), dma((NZ, NX)),
        dma((NZ,)), dma((NZ,)),
        dma((NX,)), dma((NX,)),
        dma((NZ,)), dma((NZ,)),
        dma((NZ, NX)), dma((NZ, NX)),
        dma((NZ,)), dma((NZ,)),
        dma((NZ, NX)), dma((NZ, NX)),
        dma((2, NY, 2)), dma((2, NY)),
        dma((NY,)), dma((NY,)),
        dma((NY,)), dma((NY,)),
        dma((6,)), dma((6,)),
    ]
    shapes = ((2, 16, FEAT), (HID, FEAT), (HID, FEAT))
    args = (tokens.reshape(2, 16, FEAT), grad_out.reshape(2, 16, FEAT), pre_act, w_in, w_out)
    results = pl.pallas_call(
        kernel,
        out_shape=tuple(pltpu.VMEM(shape, BF16) for shape in shapes),
        in_specs=[pl.BlockSpec(memory_space=pltpu.HBM)] * 5,
        out_specs=(pl.BlockSpec(memory_space=pltpu.VMEM),) * 3,
        scratch_shapes=scratch,
        compiler_params=pltpu.CompilerParams(
            collective_id=0, has_side_effects=True, vmem_limit_bytes=40 * 2**20
        ),
    )(*[pltpu.with_memory_space_constraint(arg, pltpu.HBM) for arg in args])
    grad_tokens, grad_w_in, grad_w_out = pl.pallas_call(
        store_kernel,
        out_shape=tuple(pltpu.HBM(shape, BF16) for shape in shapes),
        in_specs=[pl.BlockSpec(memory_space=pltpu.VMEM)] * 3,
        out_specs=(pl.BlockSpec(memory_space=pltpu.HBM),) * 3,
        scratch_shapes=[dma((3,))],
        compiler_params=pltpu.CompilerParams(vmem_limit_bytes=8 * 2**20),
    )(*[pltpu.with_memory_space_constraint(arg, pltpu.VMEM) for arg in results])
    return grad_tokens.reshape(32, FEAT), grad_w_in, grad_w_out


def solution(mesh):
    in_specs = (P("row", "col"), P("row", "col"), P("col", "row"), P("row", "col"), P("row", "col"))
    out_specs = (P("row", "col"), P("row", "col"), P("row", "col"))
    return jax.shard_map(per_device, mesh=mesh, in_specs=in_specs, out_specs=out_specs, check_vma=False)
```

```python
import jax
import jax.numpy as jnp
from jax import lax
from jax.experimental import pallas as pl
from jax.experimental.pallas import tpu as pltpu
from jax.sharding import PartitionSpec as P

tanh_scale = 0.7978845608028654
cubic_term = 0.044715

MESH = pl.DeviceIdType.MESH
F32 = jnp.float32
BF16 = jnp.bfloat16
NX, NZ, NY = 4, 4, 8
FEAT = 384
HID = 1536
HQ = HID // NX
FAR_FIRST = (4, 3, 5, 2, 6, 1, 7)
X_ORDER = (2, 1, 3)
Z_ORDER = (2, 1, 3)
A_ORDER = (1, 7, 2, 6, 4, 3, 5)
STEPS = (
    ((0, 0), (0, 1)), ((7, 0), (1, 0)), ((6, 0), (2, 0)), ((5, 0), (3, 0)),
    ((7, 1), (1, 1)), ((6, 1), (2, 1)), ((4, 0), (4, 1)), ((5, 1), (3, 1)),
)
SLOTS = {block: 2 * step + index for step, blocks in enumerate(STEPS) for index, block in enumerate(blocks)}
RELAYS = ((7, 1), (6, 2), (5, 3), (4,))
STARTS = (0, 5, 9, 13, 17)


def block_slot(d, far):
    return SLOTS[d, far]


def block_rows(d, far):
    return pl.ds(16 * block_slot(d, far), 16)


def step_rows(step):
    return pl.ds(32 * step, 32)


def gelu_hidden(u):
    q = jnp.tanh(tanh_scale * (u + cubic_term * u * u * u))
    return 0.5 * u * (1.0 + q)


def gelu_slope(u):
    q = jnp.tanh(tanh_scale * (u + cubic_term * u * u * u))
    return 0.5 * (1.0 + q) + 0.5 * u * (1.0 - q * q) * tanh_scale * (1.0 + 3.0 * cubic_term * u * u)


def kernel(
    tok_hbm, go_hbm, pre_hbm, win_hbm, wout_hbm,
    gt_out, gwi_out, gwo_out,
    tok_own, go_own, pre_own, wo2, wi2, go, go_sib, tok, pre, pre_z, part, part_f, rx, sb, rz,
    gp, gp_sib, hid, hid_sib, fb, gy,
    local, a_s, a_r, az_s, az_r, x_s, x_r, z_s, z_r, p_s, p_r, hx_s, hx_r,
    pz_s, pz_r, ex_s, ex_r, gy_s, gy_r, t_s, t_r, c_s, c_r,
):
    r, c = lax.axis_index("row"), lax.axis_index("col")
    y, zl = r // 2, r % 2
    x, zh, k = c // 8, (c // 2) % NZ, c % 2

    def dev(dy=0, dzl=0, dx=0, dz=0, core=None):
        yy, ll = (y + dy) % NY, (zl + dzl) % 2
        xx, hh = (x + dx) % NX, (zh + dz) % NZ
        kk = k if core is None else core
        return (yy * 2 + ll, (xx * NZ + hh) * 2 + kk)

    def slot(yy, ll):
        d, far = (yy + NY - y) % NY, (ll + zl) % 2
        near = jnp.minimum(d, NY - d)
        ring = 2 * near + jnp.where(d < 4, 1, 0) + far * jnp.where(near == 3, 8, 6)
        return jnp.where(near == 0, far, jnp.where(near == 4, 12 + far, ring))

    def rows(start, size):
        return pl.ds(pl.multiple_of(start, 16), size)

    def cols(index, size):
        return pl.ds(pl.multiple_of(index * size, 128), size)

    sends = []

    def send(src, dst, ssem, rsem, to):
        cp = pltpu.make_async_remote_copy(
            src_ref=src, dst_ref=dst, send_sem=ssem, recv_sem=rsem, device_id=to, device_id_type=MESH
        )
        cp.start()
        sends.append((src, ssem))

    def arrived(ref, sem):
        pltpu.make_async_copy(ref, ref, sem).wait()

    def hid_rows(xx, hh):
        return rows(16 * slot(2 * xx + hh // 2, hh % 2), 16)

    sib = dev(core=1 - k)

    peers = [dev(dy=d, core=kk) for d in range(1, NY) for kk in range(2)]
    peers += [dev(dzl=1, core=kk) for kk in range(2)] + [sib]
    peers += [dev(dx=d) for d in range(1, NX)] + [dev(dz=d) for d in range(1, NZ)]
    barrier = pltpu.get_barrier_semaphore()
    for to in peers:
        pl.semaphore_signal(barrier, inc=1, device_id=to, device_id_type=MESH)

    loads = [
        pltpu.make_async_copy(pre_hbm, pre_own, local.at[0]),
        pltpu.make_async_copy(go_hbm, go_own, local.at[1]),
        pltpu.make_async_copy(tok_hbm, tok_own, local.at[2]),
        pltpu.make_async_copy(wout_hbm, wo2.at[:, cols(k, FEAT)], local.at[3]),
        pltpu.make_async_copy(win_hbm, wi2.at[:, cols(k, FEAT)], local.at[4]),
    ]
    for cp in loads:
        cp.start()
    loads[0].wait()
    loads[1].wait()
    my_rows = hid_rows(x, zh)
    hid[my_rows, :] = gelu_hidden(pre_own[...].astype(F32)).astype(BF16)
    pre_z[zh] = pre_own[...]
    go[block_rows(0, 0), cols(k, FEAT)] = go_own[k]
    pl.semaphore_wait(barrier, len(peers))

    send(wout_hbm, wo2.at[:, cols(k, FEAT)], c_s.at[1], c_r.at[1], sib)
    send(go_own.at[1 - k], go.at[block_rows(0, 0), cols(k, FEAT)], c_s.at[0], c_r.at[0], sib)
    for kk in range(2):
        send(go_own.at[kk], go.at[block_rows(0, 1), cols(k, FEAT)], az_s.at[0, kk], az_r.at[0], dev(dzl=1, core=kk))
    for d in A_ORDER:
        for kk in range(2):
            send(
                go_own.at[kk], go.at[block_rows(d, 0), cols(k, FEAT)], a_s.at[d, kk], a_r.at[d],
                dev(dy=NY - d, core=kk),
            )
    loads[2].wait()
    tok[block_slot(0, 0)] = tok_own[...]
    send(tok_own, tok.at[block_slot(0, 1)], t_s.at[1, 0], t_r.at[1, 0], dev(dzl=1))
    for d in Z_ORDER:
        send(pre_own, pre_z.at[zh], p_s.at[d], p_r.at[d], dev(dz=d))
    for d in X_ORDER:
        send(hid.at[my_rows], hid.at[my_rows], hx_s.at[0, d], hx_r.at[0, d], dev(dx=d))

    toward = 1 - 2 * (zh % 2)
    neighbours = (toward, NZ - toward)

    def partial_sums(step):
        for d, far in STEPS[step]:
            if far:
                arrived(go.at[block_rows(d, 1), :], az_r.at[d])
            elif not d:
                arrived(go.at[block_rows(0, 0), cols(1 - k, FEAT)], c_r.at[0])
        if step == 0:
            loads[3].wait()
            arrived(wo2.at[:, cols(1 - k, FEAT)], c_r.at[1])
        t = step_rows(step)
        for dx in X_ORDER + (0,):
            xx = (x + dx) % NX
            product = lax.dot_general(
                go[t, :], wo2[rows(HQ * xx, HQ), :], (((1,), (1,)), ((), ())), preferred_element_type=F32
            )
            if dx:
                part[xx, t, :] = product.astype(BF16)
                send(part.at[xx, t], rx.at[dx - 1, t], x_s.at[step, dx], x_r.at[step, dx], dev(dx=dx))
            else:
                part_f[t, :] = product
        for d in RELAYS[step] if step < len(RELAYS) else ():
            arrived(go.at[block_rows(d, 0), :], a_r.at[d])
            send(go.at[block_rows(d, 0), :], go.at[block_rows(d, 1), :], az_s.at[d, 0], az_r.at[d], dev(dzl=1))

    def exchange(step, turn, total):
        t = step_rows(step)
        part_f[t, :] = total
        sb[turn, t, :] = total.astype(BF16)
        to = dev(dz=neighbours[(step + turn) % 2])
        send(sb.at[turn, t], rz.at[turn, t], z_s.at[step, turn], z_r.at[step, turn], to)

    def sum_over_x(step):
        t = step_rows(step)
        for dx in X_ORDER:
            arrived(rx.at[dx - 1, t], x_r.at[step, dx])
        exchange(
            step, 0, part_f[t, :] + rx[0, t, :].astype(F32) + rx[1, t, :].astype(F32) + rx[2, t, :].astype(F32)
        )

    def sum_over_pair(step):
        t = step_rows(step)
        arrived(rz.at[0, t], z_r.at[step, 0])
        exchange(step, 1, part_f[t, :] + rz[0, t, :].astype(F32))

    def times_slope(step):
        t = step_rows(step)
        slopes = []
        for d, far in STEPS[step]:
            yy, ll = (y + d) % NY, (zl + far) % 2
            slopes.append(gelu_slope(pre[yy // 2, (yy % 2) * 2 + ll].astype(F32)))
        slope = jnp.concatenate(slopes, axis=0)
        arrived(rz.at[1, t], z_r.at[step, 1])
        total = part_f[t, :] + rz[1, t, :].astype(F32)
        gp[t, cols(x, HQ)] = (total * slope).astype(BF16)
        block = gp.at[t, cols(x, HQ)]
        for dx in X_ORDER:
            send(block, block, ex_s.at[step, dx], ex_r.at[step, dx], dev(dx=dx))

    def grad_tokens_part(step):
        t = step_rows(step)
        for dx in X_ORDER:
            arrived(gp.at[t, cols((x + NX - dx) % NX, HQ)], ex_r.at[step, dx])
        fb[step] = jnp.dot(gp[t, :], wi2[...], preferred_element_type=F32).astype(BF16)
        for index, (d, far) in enumerate(STEPS[step]):
            at = pl.ds(16 * index, 16)
            for flip in range(2):
                kk = k if flip == 0 else 1 - k
                src = fb.at[step, at, cols(kk, FEAT)]
                if d or far or flip:
                    send(src, gy.at[far, d, k], gy_s.at[far, d, flip], gy_r.at[far, d], dev(dy=d, dzl=far, core=kk))
                else:
                    gy[0, 0, k] = fb[step, at, cols(kk, FEAT)]

    def hidden_on(dz):
        block = hid.at[hid_rows(x, (zh + NZ - dz) % NZ)]
        for dx in X_ORDER:
            send(block, block, hx_s.at[dz, dx], hx_r.at[dz, dx], dev(dx=dx))

    def others():
        send(go.at[:, cols(1 - k, FEAT)], go_sib, c_s.at[2], c_r.at[2], sib)
        send(win_hbm, wi2.at[:, cols(k, FEAT)], c_s.at[3], c_r.at[3], sib)
        for dz in (1, 3, 2):
            arrived(pre_z.at[(zh + NZ - dz) % NZ], p_r.at[dz])
        pre[x] = pre_z[:, :, cols(x, HQ)]
        for d in X_ORDER:
            send(pre_z.at[:, :, cols((x + d) % NX, HQ)], pre.at[x], pz_s.at[d], pz_r.at[d], dev(dx=d))
        for dz in (1, 3, 2):
            there = (zh + NZ - dz) % NZ
            hid[hid_rows(x, there), :] = gelu_hidden(pre_z[there].astype(F32)).astype(BF16)
        hidden_on(1)
        arrived(tok.at[block_slot(0, 1)], t_r.at[1, 0])
        for far in range(2):
            for d in FAR_FIRST:
                send(
                    tok.at[block_slot(0, far)], tok.at[block_slot(d, far)], t_s.at[far, d], t_r.at[far, d],
                    dev(dy=NY - d),
                )

    stages = (partial_sums, sum_over_x, sum_over_pair, times_slope, grad_tokens_part)
    for tick in range(STARTS[-1] + len(STEPS)):
        if tick == STARTS[3]:
            for d in X_ORDER:
                arrived(pre.at[(x + NX - d) % NX], pz_r.at[d])
        if tick == STARTS[4]:
            loads[4].wait()
            arrived(wi2.at[:, cols(1 - k, FEAT)], c_r.at[3])
        for index in range(len(stages)):
            if 0 <= tick - STARTS[index] < len(STEPS):
                stages[index](tick - STARTS[index])
        if tick == 7:
            others()
        if tick == STARTS[3] + 7:
            hidden_on(3)
            hidden_on(2)
    send(gp, gp_sib, c_s.at[5], c_r.at[5], sib)

    over_tokens = (((0,), (0,)), ((), ()))
    for dz in range(NZ):
        for dx in X_ORDER:
            arrived(hid.at[hid_rows((x + NX - dx) % NX, (zh + NZ - dz) % NZ)], hx_r.at[dz, dx])
    send(hid, hid_sib, c_s.at[4], c_r.at[4], sib)
    for far in range(2):
        for d in FAR_FIRST:
            arrived(tok.at[block_slot(d, far)], t_r.at[far, d])
    arrived(gp_sib, c_r.at[5])
    tok_mine = tok[:, k].reshape(256, FEAT)
    tok_other = tok[:, 1 - k].reshape(256, FEAT)
    for h in range(0, HID, 256):
        a = lax.dot_general(gp[:, h : h + 256], tok_mine, over_tokens, preferred_element_type=F32)
        b = lax.dot_general(gp_sib[:, h : h + 256], tok_other, over_tokens, preferred_element_type=F32)
        gwi_out[h : h + 256, :] = (a + b).astype(BF16)
    arrived(go_sib, c_r.at[2])
    arrived(hid_sib, c_r.at[4])
    for h in range(0, HID, 256):
        a = lax.dot_general(hid[:, h : h + 256], go[:, cols(k, FEAT)], over_tokens, preferred_element_type=F32)
        b = lax.dot_general(hid_sib[:, h : h + 256], go_sib[...], over_tokens, preferred_element_type=F32)
        gwo_out[h : h + 256, :] = (a + b).astype(BF16)
    for src, ssem in sends:
        arrived(src, ssem)
    arrived(gy.at[0, 0, 1 - k], gy_r.at[0, 0])
    total = gy[0, 0].astype(F32)
    for far in range(2):
        for d in FAR_FIRST + ((0,) if far else ()):
            arrived(gy.at[far, d], gy_r.at[far, d])
            total += gy[far, d].astype(F32)
    gt_out[...] = total.astype(BF16)


def store_kernel(*refs):
    sem = refs[-1]
    copies = [pltpu.make_async_copy(refs[i], refs[3 + i], sem.at[i]) for i in range(3)]
    for cp in copies:
        cp.start()
    for cp in copies:
        cp.wait()


def per_device(tokens, grad_out, pre_act, w_in, w_out):
    vmem = pltpu.VMEM
    dma = pltpu.SemaphoreType.DMA
    any_space = pl.BlockSpec(memory_space=pl.ANY)
    scratch = [
        vmem((2, 16, FEAT), BF16),
        vmem((2, 16, FEAT), BF16),
        vmem((16, HID), BF16),
        vmem((HID, 2 * FEAT), BF16),
        vmem((HID, 2 * FEAT), BF16),
        vmem((256, 2 * FEAT), BF16),
        vmem((256, FEAT), BF16),
        vmem((16, 2, 16, FEAT), BF16),
        vmem((NX, NZ, 16, HQ), BF16),
        vmem((NZ, 16, HID), BF16),
        vmem((NX, 256, HQ), BF16),
        vmem((256, HQ), F32),
        vmem((NX - 1, 256, HQ), BF16),
        vmem((2, 256, HQ), BF16),
        vmem((2, 256, HQ), BF16),
        vmem((256, HID), BF16),
        vmem((256, HID), BF16),
        vmem((256, HID), BF16),
        vmem((256, HID), BF16),
        vmem((8, 32, 2 * FEAT), BF16),
        vmem((2, NY, 2, 16, FEAT), BF16),
        dma((5,)),
        dma((NY, 2)), dma((NY,)),
        dma((NY, 2)), dma((NY,)),
        dma((8, NX)), dma((8, NX)),
        dma((8, 2)), dma((8, 2)),
        dma((NX,)), dma((NX,)),
        dma((NZ, NX)), dma((NZ, NX)),
        dma((NX,)), dma((NX,)),
        dma((8, NX)), dma((8, NX)),
        dma((2, NY, 2)), dma((2, NY)),
        dma((2, NY)), dma((2, NY)),
        dma((6,)), dma((6,)),
    ]
    shapes = ((2, 16, FEAT), (HID, FEAT), (HID, FEAT))
    args = (tokens.reshape(2, 16, FEAT), grad_out.reshape(2, 16, FEAT), pre_act, w_in, w_out)
    results = pl.pallas_call(
        kernel,
        out_shape=tuple(pltpu.VMEM(shape, BF16) for shape in shapes),
        in_specs=[pl.BlockSpec(memory_space=pltpu.HBM)] * 5,
        out_specs=(pl.BlockSpec(memory_space=pltpu.VMEM),) * 3,
        scratch_shapes=scratch,
        compiler_params=pltpu.CompilerParams(
            collective_id=0, has_side_effects=True, vmem_limit_bytes=40 * 2**20
        ),
    )(*[pltpu.with_memory_space_constraint(arg, pltpu.HBM) for arg in args])
    grad_tokens, grad_w_in, grad_w_out = pl.pallas_call(
        store_kernel,
        out_shape=tuple(pltpu.HBM(shape, BF16) for shape in shapes),
        in_specs=[pl.BlockSpec(memory_space=pltpu.VMEM)] * 3,
        out_specs=(pl.BlockSpec(memory_space=pltpu.HBM),) * 3,
        scratch_shapes=[dma((3,))],
        compiler_params=pltpu.CompilerParams(vmem_limit_bytes=8 * 2**20),
    )(*[pltpu.with_memory_space_constraint(arg, pltpu.VMEM) for arg in results])
    return grad_tokens.reshape(32, FEAT), grad_w_in, grad_w_out


def solution(mesh):
    in_specs = (P("row", "col"), P("row", "col"), P("col", "row"), P("row", "col"), P("row", "col"))
    out_specs = (P("row", "col"), P("row", "col"), P("row", "col"))
    return jax.shard_map(per_device, mesh=mesh, in_specs=in_specs, out_specs=out_specs, check_vma=False)
```

```python
import jax
import jax.numpy as jnp
from jax import lax
from jax.experimental import pallas as pl
from jax.experimental.pallas import tpu as pltpu
from jax.sharding import PartitionSpec as P

tanh_scale = 0.7978845608028654
cubic_term = 0.044715

MESH = pl.DeviceIdType.MESH
F32 = jnp.float32
BF16 = jnp.bfloat16
NX, NZ, NY = 4, 4, 8
FEAT = 384
HID = 1536
HQ = HID // NX
FAR_FIRST = (4, 3, 5, 2, 6, 1, 7)
X_ORDER = (2, 1, 3)
Z_ORDER = (2, 1, 3)
A_ORDER = (1, 7, 2, 6, 4, 3, 5)
STEPS = (
    ((0, 0), (0, 1)), ((7, 0), (1, 0)), ((6, 0), (2, 0)), ((5, 0), (3, 0)),
    ((7, 1), (1, 1)), ((6, 1), (2, 1)), ((4, 0), (4, 1)), ((5, 1), (3, 1)),
)
SLOTS = {block: 2 * step + index for step, blocks in enumerate(STEPS) for index, block in enumerate(blocks)}
RELAYS = ((7, 1), (6, 2), (5, 3), (4,))
STARTS = (0, 5, 9, 13, 17)


def block_slot(d, far):
    return SLOTS[d, far]


def block_rows(d, far):
    return pl.ds(16 * block_slot(d, far), 16)


def step_rows(step):
    return pl.ds(32 * step, 32)


def gelu_hidden(u):
    q = jnp.tanh(tanh_scale * (u + cubic_term * u * u * u))
    return 0.5 * u * (1.0 + q)


def gelu_slope(u):
    q = jnp.tanh(tanh_scale * (u + cubic_term * u * u * u))
    return 0.5 * (1.0 + q) + 0.5 * u * (1.0 - q * q) * tanh_scale * (1.0 + 3.0 * cubic_term * u * u)


def kernel(
    tok_hbm, go_hbm, pre_hbm, win_hbm, wout_hbm,
    gt_out, gwi_out, gwo_out,
    tok_own, go_own, pre_own, wo2, wi2, go, go_sib, tok, pre, pre_z, part, part_f, rx, sb, rz,
    gp, gp_sib, hid, hid_sib, fb, gy,
    local, a_s, a_r, az_s, az_r, x_s, x_r, z_s, z_r, p_s, p_r, hx_s, hx_r,
    pz_s, pz_r, ex_s, ex_r, gy_s, gy_r, t_s, t_r, c_s, c_r,
):
    r, c = lax.axis_index("row"), lax.axis_index("col")
    y, zl = r // 2, r % 2
    x, zh, k = c // 8, (c // 2) % NZ, c % 2

    def dev(dy=0, dzl=0, dx=0, dz=0, core=None):
        yy, ll = (y + dy) % NY, (zl + dzl) % 2
        xx, hh = (x + dx) % NX, (zh + dz) % NZ
        kk = k if core is None else core
        return (yy * 2 + ll, (xx * NZ + hh) * 2 + kk)

    def slot(yy, ll):
        d, far = (yy + NY - y) % NY, (ll + zl) % 2
        near = jnp.minimum(d, NY - d)
        ring = 2 * near + jnp.where(d < 4, 1, 0) + far * jnp.where(near == 3, 8, 6)
        return jnp.where(near == 0, far, jnp.where(near == 4, 12 + far, ring))

    def rows(start, size):
        return pl.ds(pl.multiple_of(start, 16), size)

    def cols(index, size):
        return pl.ds(pl.multiple_of(index * size, 128), size)

    sends = []

    def send(src, dst, ssem, rsem, to):
        cp = pltpu.make_async_remote_copy(
            src_ref=src, dst_ref=dst, send_sem=ssem, recv_sem=rsem, device_id=to, device_id_type=MESH
        )
        cp.start()
        sends.append((src, ssem))

    def arrived(ref, sem):
        pltpu.make_async_copy(ref, ref, sem).wait()

    def hid_rows(xx, hh):
        return rows(16 * slot(2 * xx + hh // 2, hh % 2), 16)

    sib = dev(core=1 - k)

    peers = [dev(dy=d, core=kk) for d in range(1, NY) for kk in range(2)]
    peers += [dev(dzl=1, core=kk) for kk in range(2)] + [sib]
    peers += [dev(dx=d) for d in range(1, NX)] + [dev(dz=d) for d in range(1, NZ)]
    barrier = pltpu.get_barrier_semaphore()
    for to in peers:
        pl.semaphore_signal(barrier, inc=1, device_id=to, device_id_type=MESH)

    loads = [
        pltpu.make_async_copy(pre_hbm, pre_own, local.at[0]),
        pltpu.make_async_copy(go_hbm, go_own, local.at[1]),
        pltpu.make_async_copy(tok_hbm, tok_own, local.at[2]),
        pltpu.make_async_copy(wout_hbm, wo2.at[:, cols(k, FEAT)], local.at[3]),
        pltpu.make_async_copy(win_hbm, wi2.at[:, cols(k, FEAT)], local.at[4]),
    ]
    for cp in loads:
        cp.start()
    loads[0].wait()
    loads[1].wait()
    my_rows = hid_rows(x, zh)
    hid[my_rows, :] = gelu_hidden(pre_own[...].astype(F32)).astype(BF16)
    pre_z[zh] = pre_own[...]
    go[block_rows(0, 0), cols(k, FEAT)] = go_own[k]
    pl.semaphore_wait(barrier, len(peers))

    send(wout_hbm, wo2.at[:, cols(k, FEAT)], c_s.at[1], c_r.at[1], sib)
    send(go_own.at[1 - k], go.at[block_rows(0, 0), cols(k, FEAT)], c_s.at[0], c_r.at[0], sib)
    for kk in range(2):
        send(go_own.at[kk], go.at[block_rows(0, 1), cols(k, FEAT)], az_s.at[0, kk], az_r.at[0], dev(dzl=1, core=kk))
    for d in A_ORDER:
        for kk in range(2):
            send(
                go_own.at[kk], go.at[block_rows(d, 0), cols(k, FEAT)], a_s.at[d, kk], a_r.at[d],
                dev(dy=NY - d, core=kk),
            )
    loads[2].wait()
    tok[block_slot(0, 0)] = tok_own[...]
    send(tok_own, tok.at[block_slot(0, 1)], t_s.at[1, 0], t_r.at[1, 0], dev(dzl=1))
    for d in Z_ORDER:
        send(pre_own, pre_z.at[zh], p_s.at[d], p_r.at[d], dev(dz=d))
    for d in X_ORDER:
        send(pre_own.at[:, cols((x + d) % NX, HQ)], pre.at[x, zh], pz_s.at[0, d], pz_r.at[0, d], dev(dx=d))
    for d in X_ORDER:
        send(hid.at[my_rows], hid.at[my_rows], hx_s.at[0, d], hx_r.at[0, d], dev(dx=d))

    toward = 1 - 2 * (zh % 2)
    neighbours = (toward, NZ - toward)

    def partial_sums(step):
        for d, far in STEPS[step]:
            if far:
                arrived(go.at[block_rows(d, 1), :], az_r.at[d])
            elif not d:
                arrived(go.at[block_rows(0, 0), cols(1 - k, FEAT)], c_r.at[0])
        if step == 0:
            loads[3].wait()
            arrived(wo2.at[:, cols(1 - k, FEAT)], c_r.at[1])
        t = step_rows(step)
        for dx in X_ORDER + (0,):
            xx = (x + dx) % NX
            product = lax.dot_general(
                go[t, :], wo2[rows(HQ * xx, HQ), :], (((1,), (1,)), ((), ())), preferred_element_type=F32
            )
            if dx:
                part[xx, t, :] = product.astype(BF16)
                send(part.at[xx, t], rx.at[dx - 1, t], x_s.at[step, dx], x_r.at[step, dx], dev(dx=dx))
            else:
                part_f[t, :] = product
        for d in RELAYS[step] if step < len(RELAYS) else ():
            arrived(go.at[block_rows(d, 0), :], a_r.at[d])
            send(go.at[block_rows(d, 0), :], go.at[block_rows(d, 1), :], az_s.at[d, 0], az_r.at[d], dev(dzl=1))

    def exchange(step, turn, total):
        t = step_rows(step)
        part_f[t, :] = total
        sb[turn, t, :] = total.astype(BF16)
        to = dev(dz=neighbours[(step + turn) % 2])
        send(sb.at[turn, t], rz.at[turn, t], z_s.at[step, turn], z_r.at[step, turn], to)

    def sum_over_x(step):
        t = step_rows(step)
        for dx in X_ORDER:
            arrived(rx.at[dx - 1, t], x_r.at[step, dx])
        exchange(
            step, 0, part_f[t, :] + rx[0, t, :].astype(F32) + rx[1, t, :].astype(F32) + rx[2, t, :].astype(F32)
        )

    def sum_over_pair(step):
        t = step_rows(step)
        arrived(rz.at[0, t], z_r.at[step, 0])
        exchange(step, 1, part_f[t, :] + rz[0, t, :].astype(F32))

    def times_slope(step):
        t = step_rows(step)
        slopes = []
        for d, far in STEPS[step]:
            yy, ll = (y + d) % NY, (zl + far) % 2
            slopes.append(gelu_slope(pre[yy // 2, (yy % 2) * 2 + ll].astype(F32)))
        slope = jnp.concatenate(slopes, axis=0)
        arrived(rz.at[1, t], z_r.at[step, 1])
        total = part_f[t, :] + rz[1, t, :].astype(F32)
        gp[t, cols(x, HQ)] = (total * slope).astype(BF16)
        block = gp.at[t, cols(x, HQ)]
        for dx in X_ORDER:
            send(block, block, ex_s.at[step, dx], ex_r.at[step, dx], dev(dx=dx))

    def grad_tokens_part(step):
        t = step_rows(step)
        for dx in X_ORDER:
            arrived(gp.at[t, cols((x + NX - dx) % NX, HQ)], ex_r.at[step, dx])
        fb[step] = jnp.dot(gp[t, :], wi2[...], preferred_element_type=F32).astype(BF16)
        for index, (d, far) in enumerate(STEPS[step]):
            at = pl.ds(16 * index, 16)
            for flip in range(2):
                kk = k if flip == 0 else 1 - k
                src = fb.at[step, at, cols(kk, FEAT)]
                if d or far or flip:
                    send(src, gy.at[far, d, k], gy_s.at[far, d, flip], gy_r.at[far, d], dev(dy=d, dzl=far, core=kk))
                else:
                    gy[0, 0, k] = fb[step, at, cols(kk, FEAT)]

    def hidden_on(dz):
        block = hid.at[hid_rows(x, (zh + NZ - dz) % NZ)]
        for dx in X_ORDER:
            send(block, block, hx_s.at[dz, dx], hx_r.at[dz, dx], dev(dx=dx))

    def others():
        send(go.at[:, cols(1 - k, FEAT)], go_sib, c_s.at[2], c_r.at[2], sib)
        send(win_hbm, wi2.at[:, cols(k, FEAT)], c_s.at[3], c_r.at[3], sib)
        for dz in (1, 3, 2):
            arrived(pre_z.at[(zh + NZ - dz) % NZ], p_r.at[dz])
        pre[x] = pre_z[:, :, cols(x, HQ)]
        for dz in (1, 3, 2):
            there = (zh + NZ - dz) % NZ
            for d in X_ORDER:
                src = pre_z.at[there, :, cols((x + d) % NX, HQ)]
                send(src, pre.at[x, there], pz_s.at[dz, d], pz_r.at[dz, d], dev(dx=d))
        for dz in (1, 3, 2):
            there = (zh + NZ - dz) % NZ
            hid[hid_rows(x, there), :] = gelu_hidden(pre_z[there].astype(F32)).astype(BF16)
        hidden_on(1)
        arrived(tok.at[block_slot(0, 1)], t_r.at[1, 0])
        for far in range(2):
            for d in FAR_FIRST:
                send(
                    tok.at[block_slot(0, far)], tok.at[block_slot(d, far)], t_s.at[far, d], t_r.at[far, d],
                    dev(dy=NY - d),
                )

    stages = (partial_sums, sum_over_x, sum_over_pair, times_slope, grad_tokens_part)
    for tick in range(STARTS[-1] + len(STEPS)):
        if tick == STARTS[3]:
            for dz in range(NZ):
                for d in X_ORDER:
                    arrived(pre.at[(x + NX - d) % NX, (zh + NZ - dz) % NZ], pz_r.at[dz, d])
        if tick == STARTS[4]:
            loads[4].wait()
            arrived(wi2.at[:, cols(1 - k, FEAT)], c_r.at[3])
        for index in range(len(stages)):
            if 0 <= tick - STARTS[index] < len(STEPS):
                stages[index](tick - STARTS[index])
        if tick == 7:
            others()
        if tick == STARTS[3] + 7:
            hidden_on(3)
            hidden_on(2)
    send(gp, gp_sib, c_s.at[5], c_r.at[5], sib)

    over_tokens = (((0,), (0,)), ((), ()))
    for dz in range(NZ):
        for dx in X_ORDER:
            arrived(hid.at[hid_rows((x + NX - dx) % NX, (zh + NZ - dz) % NZ)], hx_r.at[dz, dx])
    send(hid, hid_sib, c_s.at[4], c_r.at[4], sib)
    for far in range(2):
        for d in FAR_FIRST:
            arrived(tok.at[block_slot(d, far)], t_r.at[far, d])
    arrived(gp_sib, c_r.at[5])
    tok_mine = tok[:, k].reshape(256, FEAT)
    tok_other = tok[:, 1 - k].reshape(256, FEAT)
    for h in range(0, HID, 256):
        a = lax.dot_general(gp[:, h : h + 256], tok_mine, over_tokens, preferred_element_type=F32)
        b = lax.dot_general(gp_sib[:, h : h + 256], tok_other, over_tokens, preferred_element_type=F32)
        gwi_out[h : h + 256, :] = (a + b).astype(BF16)
    arrived(go_sib, c_r.at[2])
    arrived(hid_sib, c_r.at[4])
    for h in range(0, HID, 256):
        a = lax.dot_general(hid[:, h : h + 256], go[:, cols(k, FEAT)], over_tokens, preferred_element_type=F32)
        b = lax.dot_general(hid_sib[:, h : h + 256], go_sib[...], over_tokens, preferred_element_type=F32)
        gwo_out[h : h + 256, :] = (a + b).astype(BF16)
    for src, ssem in sends:
        arrived(src, ssem)
    arrived(gy.at[0, 0, 1 - k], gy_r.at[0, 0])
    total = gy[0, 0].astype(F32)
    for far in range(2):
        for d in FAR_FIRST + ((0,) if far else ()):
            arrived(gy.at[far, d], gy_r.at[far, d])
            total += gy[far, d].astype(F32)
    gt_out[...] = total.astype(BF16)


def store_kernel(*refs):
    sem = refs[-1]
    copies = [pltpu.make_async_copy(refs[i], refs[3 + i], sem.at[i]) for i in range(3)]
    for cp in copies:
        cp.start()
    for cp in copies:
        cp.wait()


def per_device(tokens, grad_out, pre_act, w_in, w_out):
    vmem = pltpu.VMEM
    dma = pltpu.SemaphoreType.DMA
    any_space = pl.BlockSpec(memory_space=pl.ANY)
    scratch = [
        vmem((2, 16, FEAT), BF16),
        vmem((2, 16, FEAT), BF16),
        vmem((16, HID), BF16),
        vmem((HID, 2 * FEAT), BF16),
        vmem((HID, 2 * FEAT), BF16),
        vmem((256, 2 * FEAT), BF16),
        vmem((256, FEAT), BF16),
        vmem((16, 2, 16, FEAT), BF16),
        vmem((NX, NZ, 16, HQ), BF16),
        vmem((NZ, 16, HID), BF16),
        vmem((NX, 256, HQ), BF16),
        vmem((256, HQ), F32),
        vmem((NX - 1, 256, HQ), BF16),
        vmem((2, 256, HQ), BF16),
        vmem((2, 256, HQ), BF16),
        vmem((256, HID), BF16),
        vmem((256, HID), BF16),
        vmem((256, HID), BF16),
        vmem((256, HID), BF16),
        vmem((8, 32, 2 * FEAT), BF16),
        vmem((2, NY, 2, 16, FEAT), BF16),
        dma((5,)),
        dma((NY, 2)), dma((NY,)),
        dma((NY, 2)), dma((NY,)),
        dma((8, NX)), dma((8, NX)),
        dma((8, 2)), dma((8, 2)),
        dma((NX,)), dma((NX,)),
        dma((NZ, NX)), dma((NZ, NX)),
        dma((NZ, NX)), dma((NZ, NX)),
        dma((8, NX)), dma((8, NX)),
        dma((2, NY, 2)), dma((2, NY)),
        dma((2, NY)), dma((2, NY)),
        dma((6,)), dma((6,)),
    ]
    shapes = ((2, 16, FEAT), (HID, FEAT), (HID, FEAT))
    args = (tokens.reshape(2, 16, FEAT), grad_out.reshape(2, 16, FEAT), pre_act, w_in, w_out)
    results = pl.pallas_call(
        kernel,
        out_shape=tuple(pltpu.VMEM(shape, BF16) for shape in shapes),
        in_specs=[pl.BlockSpec(memory_space=pltpu.HBM)] * 5,
        out_specs=(pl.BlockSpec(memory_space=pltpu.VMEM),) * 3,
        scratch_shapes=scratch,
        compiler_params=pltpu.CompilerParams(
            collective_id=0, has_side_effects=True, vmem_limit_bytes=40 * 2**20
        ),
    )(*[pltpu.with_memory_space_constraint(arg, pltpu.HBM) for arg in args])
    grad_tokens, grad_w_in, grad_w_out = pl.pallas_call(
        store_kernel,
        out_shape=tuple(pltpu.HBM(shape, BF16) for shape in shapes),
        in_specs=[pl.BlockSpec(memory_space=pltpu.VMEM)] * 3,
        out_specs=(pl.BlockSpec(memory_space=pltpu.HBM),) * 3,
        scratch_shapes=[dma((3,))],
        compiler_params=pltpu.CompilerParams(vmem_limit_bytes=8 * 2**20),
    )(*[pltpu.with_memory_space_constraint(arg, pltpu.VMEM) for arg in results])
    return grad_tokens.reshape(32, FEAT), grad_w_in, grad_w_out


def solution(mesh):
    in_specs = (P("row", "col"), P("row", "col"), P("col", "row"), P("row", "col"), P("row", "col"))
    out_specs = (P("row", "col"), P("row", "col"), P("row", "col"))
    return jax.shard_map(per_device, mesh=mesh, in_specs=in_specs, out_specs=out_specs, check_vma=False)
```
